512 devices in a mesh: req: 64 (over y, z), tp: 8 (over x, core).
Axes of the slice: x: 4, y: 4, z: 16, core: 2. Of those that a mesh axis runs over, the one named last changes fastest.
Arguments:
- tail_queries: bfloat16 [128, 256, 64, 128], P('req', None, 'tp'), may hold values from -140 to 140
- tail_keys: bfloat16 [128, 256, 8, 128], P('req', 'tp'), may hold values from -6 to 6
- tail_values: bfloat16 [128, 256, 8, 128], P('req', 'tp'), may hold values from -6 to 6
- prefix_keys: bfloat16 [128, 768, 8, 128], P('req', None, 'tp'), may hold values from -4 to 4
- prefix_values: bfloat16 [128, 768, 8, 128], P('req', None, 'tp'), may hold values from -6 to 6
- decode_queries: bfloat16 [128, 4, 64, 128], P('req', None, 'tp'), may hold values from -140 to 140
- decode_keys: bfloat16 [128, 4, 8, 128], P('req', None, 'tp'), may hold values from -6 to 6
- decode_values: bfloat16 [128, 4, 8, 128], P('req', None, 'tp'), may hold values from -6 to 6
- prompt_lengths: int32 [128], P('req'), may hold values from 258 to 1024, as said below
- block_dest: int32 [128, 64, 1], P('req'), may hold values from 0 to 63; in each aligned block of 128 rows (0 to 127, 128 to 255, ..., all dimensions but the last counted through in order) at most 4 rows name the same one
Outputs:
- prefill_out: bfloat16 [128, 256, 64, 128], P('req', None, 'tp')
- decode_out: bfloat16 [128, 4, 64, 128], P('req', None, 'tp')
- pool_keys: bfloat16 [64, 256, 16, 8, 128], P('req', None, None, 'tp')
- pool_values: bfloat16 [64, 256, 16, 8, 128], P('req', None, None, 'tp')
The draws below stay inside these ranges and needn't reach their ends.
Inputs may be any that keep to these rules, and one draw needn't show every extreme that they name: `prompt_lengths`: some prompt has exactly 1024 tokens and some exactly 258. `block_dest`: among the 128 blocks of one request group, no pool group is named more than 4 times.
All inputs are finite; a program needn't handle non-finite values.
Results may differ from the reference program's by a relative error of at most 0.0046.
Values may be sent and summed in bfloat16 or wider, within the bound.
A program may use at most 64 MiB of HBM per device.

```python
import math
import jax
import jax.numpy as jnp
import numpy as np
from jax import lax

QH = 64
KVH = 8
HD = 128
P_DEV = 2
TAIL = 256
PROMPT = 1024
BLOCK = 16
STEPS = 4
PREFIX = 768
NB = 64
PROMPTS = 128
SLOTS_PEER = 4
N_REQ = 64


def shared_keys(key):
    return jnp.clip(jax.random.normal(key, (PROMPTS, PREFIX, KVH, HD), jnp.float32), -4.0, 4.0)


def draw_prefix_keys(key, part):
    row_base = shared_keys(key)
    return row_base.astype(jnp.bfloat16)


def draw_tail_queries(key, part):
    key = jax.random.fold_in(key, 7)
    return jnp.clip(jax.random.normal(key, (PROMPTS, TAIL, QH, HD), jnp.float32), -6.0, 6.0).astype(jnp.bfloat16)


def draw_decode_queries(key, part):
    key = jax.random.fold_in(key, 8)
    return jnp.clip(jax.random.normal(key, (PROMPTS, STEPS, QH, HD), jnp.float32), -6.0, 6.0).astype(jnp.bfloat16)


def draw_prompt_lengths(key, part):
    key = jax.random.fold_in(key, 9)
    first_key, second_key = jax.random.split(key)
    lengths = jax.random.randint(first_key, (PROMPTS,), TAIL + 2, PROMPT + 1)
    longest = jax.random.randint(second_key, (), 0, PROMPTS)
    prompt_index = jnp.arange(PROMPTS)
    lengths = jnp.where(prompt_index == longest, PROMPT, lengths)
    lengths = jnp.where(prompt_index == (longest + 1) % PROMPTS, TAIL + 2, lengths)
    return lengths.astype(jnp.int32)


def levels(stream_key, dims, pieces, smallest, high):
    factor_of, own = 1.0, jax.random.fold_in(stream_key, 6)
    for axis_at, parts in pieces:
        heights = jnp.exp(jax.random.uniform(jax.random.fold_in(own, axis_at), (parts,), jnp.float32, smallest / len(pieces), high / len(pieces)))
        factor_of = factor_of * jnp.repeat(heights, dims[axis_at] // parts).reshape([-1 if axis == axis_at else 1 for axis in range(len(dims))])
    return factor_of


def shared_out(key, own, number, rows, count, top, most, lean):
    ranking = jax.random.permutation(key, count)
    heavy_load, ordinary = load_shares(count, rows * top, most, lean, True), load_shares(count, rows * top, most, lean, False)
    places = jnp.arange(count)

    def named(tallies, offset_by):
        used = int((tallies > 0).sum())
        fixed = max(1, used // 4)
        moved = fixed + (places - fixed + offset_by * (used - fixed)) % max(1, count - fixed)
        return jnp.zeros((count,), jnp.int32).at[ranking[jnp.where(places < fixed, places, moved)]].set(jnp.asarray(tallies, jnp.int32))

    tallies = jnp.where(number % 4 == 0, named(heavy_load, number // 4), named(ordinary, number - number // 4 - 1))
    mixed = jax.random.permutation(jax.random.fold_in(own, 3), count)
    giver, taker = mixed[0:count // 2 * 2:2], mixed[1:count // 2 * 2:2]
    margin = jnp.minimum(tallies[giver] - 1, most - tallies[taker]) // 2
    margin = jnp.where((giver == ranking[0]) | (taker == ranking[0]) | (tallies[taker] == 0), 0, jnp.maximum(margin, 0))
    moved = jax.random.randint(jax.random.fold_in(own, 4), (count // 2,), 0, 1 << 20) % (margin + 1)
    tallies = tallies.at[giver].add(-moved).at[taker].add(moved)
    labels = jnp.searchsorted(jnp.cumsum(tallies), jnp.arange(rows * top), side="right").astype(jnp.int32)
    table = labels.reshape(top, rows).T
    table = table[jax.random.permutation(jax.random.fold_in(own, 1), rows)]
    offset_by = jax.random.randint(jax.random.fold_in(own, 2), (rows, 1), 0, top)
    return jnp.take_along_axis(table, (jnp.arange(top)[None, :] + offset_by) % top, axis=1)


def load_shares(amount, total, bound, lean, full):
    loads = [(1 << 20) // math.isqrt(standing ** lean) + 1 for standing in range(1, amount + 1)]
    largest = bound if full else min(bound, max(-(-total // amount), total * loads[0] // sum(loads)))
    least = 1 if total - largest >= amount - 1 else 0
    counts, rest = [largest] + [least] * (amount - 1), total - largest - least * (amount - 1)
    while rest > 0:
        candidates = [i for i in range(1, amount) if counts[i] < largest] or [i for i in range(1, amount) if counts[i] < bound]
        mass, budget = sum([loads[i] for i in candidates]), rest
        for i in candidates:
            extra = min(bound - counts[i], max(1, budget * loads[i] // mass), rest)
            counts[i] = counts[i] + extra
            rest = rest - extra
    return np.array(counts)


def noise(own_key, extent, scale, most, cuts=(), kind=jnp.bfloat16):
    gain = levels(own_key, extent, cuts, -0.22, 0.18) if cuts else 1.0
    array = jax.random.normal(own_key, extent, jnp.float32) * scale * gain
    return jnp.minimum(jnp.maximum(array, -most), most).astype(kind)


def setup_inputs(seed: int = 0) -> dict:
    keys = jax.random.split(jax.random.key(seed), 11)
    tail_queries = draw_tail_queries(jax.random.fold_in(keys[10], 71), 0)
    tail_keys = noise(keys[1], (PROMPTS, TAIL, KVH, HD), 1.0, 6.0, ((0, 64), (1, 8)))
    tail_values = noise(keys[2], (PROMPTS, TAIL, KVH, HD), 1.0, 6.0, ((0, 64), (1, 8)))
    prefix_keys = draw_prefix_keys(jax.random.fold_in(keys[10], 71), 0)
    prefix_values = noise(keys[4], (PROMPTS, PREFIX, KVH, HD), 1.0, 6.0, ((0, 64), (2, 8)))
    decode_queries = draw_decode_queries(jax.random.fold_in(keys[10], 71), 0)
    decode_keys = noise(keys[6], (PROMPTS, STEPS, KVH, HD), 1.0, 6.0, ((0, 64), (2, 8)))
    decode_values = noise(keys[7], (PROMPTS, STEPS, KVH, HD), 1.0, 6.0, ((0, 64), (2, 8)))
    prompt_lengths = draw_prompt_lengths(jax.random.fold_in(keys[10], 71), 0)
    block_dest_keys = jax.random.split(jax.random.fold_in(keys[9], 1), PROMPTS * NB // (P_DEV * NB))
    block_dest_turns = jax.random.permutation(jax.random.fold_in(keys[9], 3), PROMPTS * NB // (P_DEV * NB))
    block_dest = jax.vmap(lambda own, number: shared_out(jax.random.fold_in(keys[9], 2), own, number, P_DEV * NB, N_REQ, 1, SLOTS_PEER, 2))(block_dest_keys, block_dest_turns).reshape((PROMPTS, NB, 1))
    return {"tail_queries": tail_queries, "tail_keys": tail_keys, "tail_values": tail_values, "prefix_keys": prefix_keys, "prefix_values": prefix_values, "decode_queries": decode_queries, "decode_keys": decode_keys, "decode_values": decode_values, "prompt_lengths": prompt_lengths, "block_dest": block_dest}


def assemble(prefix, tail_part, length):
    zero_rows = jnp.zeros((TAIL,) + prefix.shape[1:], prefix.dtype)
    padded = jnp.concatenate([prefix, zero_rows], 0)
    placed = lax.dynamic_update_slice_in_dim(padded, tail_part, (length - TAIL).astype(jnp.int32), 0)
    position = jnp.arange(PROMPT, dtype=jnp.int32)
    return jnp.where((position < length)[:, None, None], placed, jnp.zeros_like(placed))

def rounded_copy(weights):
    narrow = lax.optimization_barrier(weights.astype(jnp.bfloat16))
    return narrow.astype(jnp.float32)

def prefill_one(items):
    queries, key_rows, value_rows, length = items
    group_size = QH // KVH
    shaped = queries.reshape(TAIL, KVH, group_size, HD).astype(jnp.float32)
    scores = jnp.einsum('tkgd,skd->kgts', shaped, key_rows.astype(jnp.float32)) * (1.0 / math.sqrt(HD))
    last_seen = length - TAIL + jnp.arange(TAIL, dtype=jnp.int32)
    visible = jnp.arange(PROMPT, dtype=jnp.int32)[None, :] <= last_seen[:, None]
    scores = jnp.where(visible, scores, -jnp.inf)
    row_peak = lax.optimization_barrier(jnp.max(scores, -1, keepdims=True))
    weights = jnp.exp(scores - row_peak)
    weight_sum = lax.optimization_barrier(jnp.sum(weights, -1))
    summed = jnp.einsum('kgts,skd->tkgd', rounded_copy(weights), value_rows.astype(jnp.float32))
    result = summed / jnp.transpose(weight_sum, (2, 0, 1))[..., None]
    return result.reshape(TAIL, QH, HD).astype(jnp.bfloat16)

def decode_one(items):
    queries, key_rows, value_rows, new_keys, new_values, length = items
    group_size = QH // KVH
    shaped = queries.reshape(STEPS, KVH, group_size, HD).astype(jnp.float32)
    inverse_root = 1.0 / math.sqrt(HD)
    prompt_scores = jnp.einsum('qkgd,skd->kgqs', shaped, key_rows.astype(jnp.float32)) * inverse_root
    prompt_scores = jnp.where(jnp.arange(PROMPT, dtype=jnp.int32) < length, prompt_scores, -jnp.inf)
    fresh_scores = jnp.einsum('qkgd,nkd->kgqn', shaped, new_keys.astype(jnp.float32)) * inverse_root
    causal = jnp.arange(STEPS)[None, :] <= jnp.arange(STEPS)[:, None]
    fresh_scores = jnp.where(causal, fresh_scores, -jnp.inf)
    row_peak = jnp.maximum(lax.optimization_barrier(jnp.max(prompt_scores, -1)), lax.optimization_barrier(jnp.max(fresh_scores, -1)))[..., None]
    prompt_weights = jnp.exp(prompt_scores - row_peak)
    fresh_weights = jnp.exp(fresh_scores - row_peak)
    weight_sum = lax.optimization_barrier(jnp.sum(prompt_weights, -1)) + lax.optimization_barrier(jnp.sum(fresh_weights, -1))
    summed = jnp.einsum('kgqs,skd->kgqd', rounded_copy(prompt_weights), value_rows.astype(jnp.float32))
    summed = summed + jnp.einsum('kgqn,nkd->kgqd', rounded_copy(fresh_weights), new_values.astype(jnp.float32))
    result = summed / weight_sum[..., None]
    return jnp.transpose(result, (2, 0, 1, 3)).reshape(STEPS, QH, HD).astype(jnp.bfloat16)

def build_pool(whole, block_dest):
    per_source = P_DEV * NB
    blocks = whole.reshape(N_REQ, per_source, BLOCK, KVH, HD)
    target = block_dest.reshape(N_REQ, per_source)
    onehot = (target[:, :, None] == jnp.arange(N_REQ, dtype=jnp.int32)[None, None, :]).astype(jnp.int32)
    block_rank = lax.optimization_barrier(jnp.sum((jnp.cumsum(onehot, 1) - onehot) * onehot, 2))
    column = jnp.arange(N_REQ, dtype=jnp.int32)[:, None] * SLOTS_PEER + block_rank
    empty_pool = jnp.zeros((N_REQ, N_REQ * SLOTS_PEER, BLOCK, KVH, HD), whole.dtype)
    return empty_pool.at[target, column].set(blocks)

def reference(tail_queries, tail_keys, tail_values, prefix_keys, prefix_values, decode_queries, decode_keys, decode_values, prompt_lengths, block_dest):
    whole_keys = jax.vmap(assemble)(prefix_keys, tail_keys, prompt_lengths)
    whole_values = jax.vmap(assemble)(prefix_values, tail_values, prompt_lengths)
    prefill_out = lax.map(prefill_one, (tail_queries, whole_keys, whole_values, prompt_lengths))
    decode_out = lax.map(decode_one, (decode_queries, whole_keys, whole_values, decode_keys, decode_values, prompt_lengths))
    pool_keys = build_pool(whole_keys, block_dest)
    pool_values = build_pool(whole_values, block_dest)
    return (prefill_out, decode_out, pool_keys, pool_values)
```

```python
import functools
import math

import jax
import jax.numpy as jnp
from jax import lax
from jax.experimental import pallas as pl
from jax.experimental.pallas import tpu as pltpu
from jax.sharding import PartitionSpec as P

MESH = pl.DeviceIdType.MESH
BLOCK = 16
SLOTS = 4
Y = 4
F32 = jnp.float32
BF16 = jnp.bfloat16


def iota(shape, dim):
    return lax.broadcasted_iota(jnp.int32, shape, dim)


def dot(a, b):
    return jnp.dot(a, b, preferred_element_type=F32)


def dot_t(a, b):
    return lax.dot_general(a, b, (((1,), (1,)), ((), ())), preferred_element_type=F32)


def slot_table(dest_row, slots, empty):
    count = dest_row.shape[1]
    by_lane = jnp.broadcast_to(dest_row, (count, count))
    by_row = by_lane.T
    earlier = iota((count, count), 1) < iota((count, count), 0)
    rank = jnp.sum(jnp.where((by_lane == by_row) & earlier, 1, 0), axis=1, keepdims=True)
    slot = by_row[:, :1] * SLOTS + rank
    held = slot == iota((count, slots), 1)
    block = iota((count, slots), 0) - empty
    return jnp.sum(jnp.where(held, block, 0), axis=0, keepdims=True) + empty


def exchange_kernel(
    groups,
    heads,
    tk_in,
    tv_in,
    dest_in,
    len_in,
    pk_in,
    pv_in,
    q_in,
    dq_in,
    dk_in,
    dv_in,
    out_ref,
    dout_ref,
    pool_ref,
    tk_ref,
    tv_ref,
    dest_ref,
    len_ref,
    pk_ref,
    pv_ref,
    q_ref,
    dq_ref,
    dk_ref,
    dv_ref,
    tsend,
    trecv,
    tail,
    wk,
    wv,
    send,
    tab_v,
    tab_s,
    tail_ssem,
    tail_rsem,
    ssem,
    rsem,
    lsem,
    isem,
):
    prompts, tail_len, group, hd = q_ref.shape
    tokens = tk_ref.shape[1]
    prefix_len = pk_ref.shape[1]
    whole_len = prefix_len + tail_len
    per_prompt = whole_len // BLOCK
    blocks = prompts * per_prompt
    me = lax.axis_index("req")
    tp = lax.axis_index("tp")
    nz = groups // Y
    my_y, my_z = me // nz, me % nz

    def partner(d):
        return lax.rem(my_y + d // nz, Y) * nz + lax.rem(my_z + d % nz, nz)

    loads = [
        pltpu.make_async_copy(source, target, isem.at[i])
        for i, (source, target) in enumerate(
            (
                (tk_in, tk_ref),
                (tv_in, tv_ref),
                (dest_in, dest_ref),
                (len_in, len_ref),
                (pk_in, pk_ref),
                (pv_in, pv_ref),
                (q_in, q_ref),
                (dq_in, dq_ref),
                (dk_in, dk_ref),
                (dv_in, dv_ref),
            )
        )
    ]
    for load in loads:
        load.start()

    barrier = pltpu.get_barrier_semaphore()
    for d in range(1, heads):
        other = lax.rem(tp + d, heads)
        pl.semaphore_signal(barrier, inc=1, device_id=(me, other), device_id_type=MESH)

    def greet(d, carry):
        pl.semaphore_signal(barrier, inc=1, device_id=(partner(d), tp), device_id_type=MESH)
        return carry

    lax.fori_loop(1, groups, greet, 0)

    rows = prompts * tokens * heads
    per_head = prompts * tokens
    row, column = iota((rows, rows), 0), iota((rows, rows), 1)
    wanted = lax.rem(row, per_head) * heads + lax.div(row, per_head)
    pick = jnp.where(column == wanted, 1.0, 0.0).astype(BF16)
    loads[0].wait()
    loads[1].wait()
    flat = jnp.concatenate([tk_ref[...].reshape(rows, hd), tv_ref[...].reshape(rows, hd)], axis=1)
    tsend[...] = dot(pick, flat).astype(BF16).reshape(heads, per_head, 2 * hd)

    loads[2].wait()
    dest_row = jnp.concatenate([dest_ref[p] for p in range(prompts)], axis=1)
    tab_v[...] = slot_table(dest_row, groups * SLOTS, blocks)
    table_copy = pltpu.make_async_copy(tab_v, tab_s, lsem.at[0])
    table_copy.start()

    pl.semaphore_wait(barrier, heads - 1 + groups - 1)

    tail_copies = []
    for d in range(1, heads):
        other = lax.rem(tp + d, heads)
        copy = pltpu.make_async_remote_copy(
            src_ref=tsend.at[other],
            dst_ref=trecv.at[tp],
            send_sem=tail_ssem.at[d],
            recv_sem=tail_rsem.at[d],
            device_id=(me, other),
            device_id_type=MESH,
        )
        copy.start()
        tail_copies.append(copy)
    own_tail = pltpu.make_async_copy(tsend.at[tp], trecv.at[tp], lsem.at[1])
    own_tail.start()
    wk[blocks] = jnp.zeros((BLOCK, hd), BF16)
    wv[blocks] = jnp.zeros((BLOCK, hd), BF16)
    table_copy.wait()
    for load in loads[3:6]:
        load.wait()
    own_tail.wait()
    for copy in tail_copies:
        copy.wait()

    for p in range(prompts):
        for s in range(heads):
            tail[p, s * tokens : (s + 1) * tokens] = trecv[s, p * tokens : (p + 1) * tokens]
    chunk = 128
    for p in range(prompts):
        start = len_ref[p] - tail_len
        for c in range(whole_len // chunk):
            row = iota((chunk, tail_len), 0) + c * chunk
            shift = jnp.where(iota((chunk, tail_len), 1) == row - start, 1.0, 0.0).astype(BF16)
            moved = dot(shift, tail[p])
            moved_k, moved_v = moved[:, :hd], moved[:, hd:]
            if c * chunk < prefix_len:
                early = iota((chunk, hd), 0) + c * chunk < start
                at = slice(c * chunk, (c + 1) * chunk)
                moved_k = jnp.where(early, pk_ref[p, at].astype(F32), moved_k)
                moved_v = jnp.where(early, pv_ref[p, at].astype(F32), moved_v)
            first = (p * whole_len + c * chunk) // BLOCK
            shape = (chunk // BLOCK, BLOCK, hd)
            wk[first : first + chunk // BLOCK] = moved_k.astype(BF16).reshape(shape)
            wv[first : first + chunk // BLOCK] = moved_v.astype(BF16).reshape(shape)

    def pack(target):
        for r in range(SLOTS):
            block = tab_s[0, target * SLOTS + r]
            send[target, 0, r] = wk[block]
            send[target, 1, r] = wv[block]

    def pool_copy(d):
        target = partner(d)
        return pltpu.make_async_remote_copy(
            src_ref=send.at[target],
            dst_ref=pool_ref.at[me],
            send_sem=ssem.at[d],
            recv_sem=rsem.at[d],
            device_id=(target, tp),
            device_id_type=MESH,
        )

    def ship(d, carry):
        pack(partner(d))
        pool_copy(d).start()
        return carry

    lax.fori_loop(1, groups, ship, 0)
    pack(me)
    own_pool = pltpu.make_async_copy(send.at[me], pool_ref.at[me], lsem.at[2])
    own_pool.start()

    for load in loads[6:]:
        load.wait()
    scale = 1.0 / math.sqrt(hd)
    chunk_tokens = 32
    chunk_rows = chunk_tokens * group
    for p in range(prompts):
        length = len_ref[p]

        def keys_of(whole):
            return whole[p * per_prompt : (p + 1) * per_prompt].reshape(whole_len, hd)

        def prefill(c, carry):
            first = pl.multiple_of(c * chunk_tokens, chunk_tokens)
            q = q_ref[p, pl.ds(first, chunk_tokens)].reshape(chunk_rows, hd)
            scores = dot_t(q, keys_of(wk)) * scale
            token = lax.div(iota((chunk_rows, whole_len), 0), group)
            last = length - tail_len + first + token
            scores = jnp.where(iota((chunk_rows, whole_len), 1) <= last, scores, -jnp.inf)
            peak = jnp.max(scores, axis=1, keepdims=True)
            weights = jnp.exp(scores - peak)
            total = jnp.sum(weights, axis=1, keepdims=True)
            summed = dot(weights.astype(BF16), keys_of(wv))
            result = (summed / total).astype(BF16)
            out_ref[p, pl.ds(first, chunk_tokens)] = result.reshape(chunk_tokens, group, hd)
            return carry

        lax.fori_loop(0, tail_len // chunk_tokens, prefill, 0)

        steps = dq_ref.shape[1]
        dq = dq_ref[p].reshape(steps * group, hd)
        scores = dot_t(dq, keys_of(wk)) * scale
        scores = jnp.where(iota(scores.shape, 1) < length, scores, -jnp.inf)
        fresh = dot_t(dq, dk_ref[p]) * scale
        step = lax.div(iota(fresh.shape, 0), group)
        fresh = jnp.where(iota(fresh.shape, 1) <= step, fresh, -jnp.inf)
        peak = jnp.maximum(
            jnp.max(scores, axis=1, keepdims=True), jnp.max(fresh, axis=1, keepdims=True)
        )
        weights = jnp.exp(scores - peak)
        fresh_weights = jnp.exp(fresh - peak)
        total = jnp.sum(weights, axis=1, keepdims=True) + jnp.sum(
            fresh_weights, axis=1, keepdims=True
        )
        summed = dot(weights.astype(BF16), keys_of(wv))
        summed = summed + dot(fresh_weights.astype(BF16), dv_ref[p])
        dout_ref[p] = (summed / total).astype(BF16).reshape(steps, group, hd)

    own_pool.wait()

    def finish(d, carry):
        pool_copy(d).wait()
        return carry

    lax.fori_loop(1, groups, finish, 0)


def store_kernel(pool_ref, out_ref, dout_ref, pk_ref, pv_ref, o_ref, do_ref, sem):
    copies = [
        pltpu.make_async_copy(pool_ref.at[:, 0], pk_ref, sem.at[0]),
        pltpu.make_async_copy(pool_ref.at[:, 1], pv_ref, sem.at[1]),
        pltpu.make_async_copy(out_ref, o_ref, sem.at[2]),
        pltpu.make_async_copy(dout_ref, do_ref, sem.at[3]),
    ]
    for copy in copies:
        copy.start()
    for copy in copies:
        copy.wait()


def per_device(groups, heads, tq, tk, tv, pk, pv, dq, dk, dv, lengths, dest):
    prompts, tail_len, group, hd = tq.shape
    tokens = tk.shape[1]
    prefix_len = pk.shape[1]
    steps = dq.shape[1]
    blocks = prompts * (prefix_len + tail_len) // BLOCK
    vmem = pl.BlockSpec(memory_space=pltpu.VMEM)
    hbm = pl.BlockSpec(memory_space=pltpu.HBM)
    shape = jax.ShapeDtypeStruct
    operands = (
        tk,
        tv,
        dest.reshape(prompts, 1, dest.shape[1]),
        lengths,
        pk.reshape(prompts, prefix_len, hd),
        pv.reshape(prompts, prefix_len, hd),
        tq,
        dq,
        dk.reshape(prompts, steps, hd),
        dv.reshape(prompts, steps, hd),
    )
    held = [pltpu.VMEM(x.shape, x.dtype) for x in operands]
    held[3] = pltpu.SMEM(lengths.shape, lengths.dtype)
    out, dout, pool = pl.pallas_call(
        functools.partial(exchange_kernel, groups, heads),
        out_shape=(
            pltpu.VMEM(tq.shape, BF16),
            pltpu.VMEM(dq.shape, BF16),
            pltpu.VMEM((groups, 2, SLOTS, BLOCK, hd), BF16),
        ),
        in_specs=[hbm] * len(operands),
        out_specs=(vmem, vmem, vmem),
        scratch_shapes=held
        + [
            pltpu.VMEM((heads, prompts * tokens, 2 * hd), BF16),
            pltpu.VMEM((heads, prompts * tokens, 2 * hd), BF16),
            pltpu.VMEM((prompts, tail_len, 2 * hd), BF16),
            pltpu.VMEM((blocks + 1, BLOCK, hd), BF16),
            pltpu.VMEM((blocks + 1, BLOCK, hd), BF16),
            pltpu.VMEM((groups, 2, SLOTS, BLOCK, hd), BF16),
            pltpu.VMEM((1, groups * SLOTS), jnp.int32),
            pltpu.SMEM((1, groups * SLOTS), jnp.int32),
            pltpu.SemaphoreType.DMA((heads,)),
            pltpu.SemaphoreType.DMA((heads,)),
            pltpu.SemaphoreType.DMA((groups,)),
            pltpu.SemaphoreType.DMA((groups,)),
            pltpu.SemaphoreType.DMA((3,)),
            pltpu.SemaphoreType.DMA((len(operands),)),
        ],
        compiler_params=pltpu.CompilerParams(
            collective_id=0, has_side_effects=True, vmem_limit_bytes=40 << 20
        ),
    )(*[pltpu.with_memory_space_constraint(x, pltpu.HBM) for x in operands])
    pool_k, pool_v, out, dout = pl.pallas_call(
        store_kernel,
        out_shape=(
            shape((groups, SLOTS, BLOCK, hd), BF16),
            shape((groups, SLOTS, BLOCK, hd), BF16),
            shape(tq.shape, BF16),
            shape(dq.shape, BF16),
        ),
        in_specs=[vmem] * 3,
        out_specs=(hbm,) * 4,
        scratch_shapes=[pltpu.SemaphoreType.DMA((4,))],
        compiler_params=pltpu.CompilerParams(vmem_limit_bytes=40 << 20),
    )(pool, out, dout)
    final = (1, groups * SLOTS, BLOCK, 1, hd)
    return out, dout, pool_k.reshape(final), pool_v.reshape(final)


def solution(mesh):
    in_specs = (
        P("req", None, "tp", None),
        P("req", "tp", None, None),
        P("req", "tp", None, None),
        P("req", None, "tp", None),
        P("req", None, "tp", None),
        P("req", None, "tp", None),
        P("req", None, "tp", None),
        P("req", None, "tp", None),
        P("req"),
        P("req", None, None),
    )
    out_specs = (
        P("req", None, "tp", None),
        P("req", None, "tp", None),
        P("req", None, None, "tp", None),
        P("req", None, None, "tp", None),
    )
    return jax.shard_map(
        functools.partial(per_device, mesh.shape["req"], mesh.shape["tp"]),
        mesh=mesh,
        in_specs=in_specs,
        out_specs=out_specs,
        check_vma=False,
    )
```

```python
import functools
import math

import jax
import jax.numpy as jnp
from jax import lax
from jax.experimental import pallas as pl
from jax.experimental.pallas import tpu as pltpu
from jax.sharding import PartitionSpec as P

MESH = pl.DeviceIdType.MESH
BLOCK = 16
SLOTS = 4
Y = 4
F32 = jnp.float32
BF16 = jnp.bfloat16


def iota(shape, dim):
    return lax.broadcasted_iota(jnp.int32, shape, dim)


def dot(a, b):
    return jnp.dot(a, b, preferred_element_type=F32)


def dot_t(a, b):
    return lax.dot_general(a, b, (((1,), (1,)), ((), ())), preferred_element_type=F32)


def slot_table(dest_row, slots, empty):
    count = dest_row.shape[1]
    by_lane = jnp.broadcast_to(dest_row, (count, count))
    by_row = by_lane.T
    earlier = iota((count, count), 1) < iota((count, count), 0)
    rank = jnp.sum(jnp.where((by_lane == by_row) & earlier, 1, 0), axis=1, keepdims=True)
    slot = by_row[:, :1] * SLOTS + rank
    held = slot == iota((count, slots), 1)
    block = iota((count, slots), 0) - empty
    return jnp.sum(jnp.where(held, block, 0), axis=0, keepdims=True) + empty


def exchange_kernel(
    groups,
    heads,
    tk_in,
    tv_in,
    dest_in,
    len_in,
    pk_in,
    pv_in,
    q_in,
    dq_in,
    dk_in,
    dv_in,
    out_ref,
    dout_ref,
    pool_ref,
    tk_ref,
    tv_ref,
    dest_ref,
    len_ref,
    pk_ref,
    pv_ref,
    q_ref,
    dq_ref,
    dk_ref,
    dv_ref,
    tsend,
    tail,
    shift,
    wk,
    wv,
    send,
    tab_v,
    tab_s,
    tail_ssem,
    tail_rsem,
    ssem,
    rsem,
    tab_sem,
    own_sem,
    isem,
):
    prompts, tail_len, group, hd = q_ref.shape
    tokens = tk_ref.shape[1]
    prefix_len = pk_ref.shape[1]
    whole_len = prefix_len + tail_len
    per_prompt = whole_len // BLOCK
    blocks = prompts * per_prompt
    me = lax.axis_index("req")
    tp = lax.axis_index("tp")
    nz = groups // Y
    my_y, my_z = me // nz, me % nz

    along_y = [lax.rem(my_y + dy, Y) * nz for dy in range(Y)]

    def partner(dy, dz):
        return along_y[dy] + lax.rem(my_z + dz, nz)

    loads = [
        pltpu.make_async_copy(source, target, isem.at[i])
        for i, (source, target) in enumerate(
            (
                (tk_in, tk_ref),
                (tv_in, tv_ref),
                (dest_in, dest_ref),
                (len_in, len_ref),
                (pk_in, pk_ref),
                (pv_in, pv_ref),
                (q_in, q_ref),
                (dq_in, dq_ref),
                (dk_in, dk_ref),
                (dv_in, dv_ref),
            )
        )
    ]
    for load in loads[:3]:
        load.start()

    barrier = pltpu.get_barrier_semaphore()
    for d in range(1, heads):
        other = lax.rem(tp + d, heads)
        pl.semaphore_signal(barrier, inc=1, device_id=(me, other), device_id_type=MESH)

    for dy in range(Y):
        for dz in range(nz):
            if dy or dz:
                pl.semaphore_signal(
                    barrier, inc=1, device_id=(partner(dy, dz), tp), device_id_type=MESH
                )
    for load in loads[3:]:
        load.start()

    rows = prompts * tokens * heads
    per_head = prompts * tokens
    row, column = iota((rows, rows), 0), iota((rows, rows), 1)
    wanted = (row & (per_head - 1)) * heads + (row >> (per_head.bit_length() - 1))
    pick = jnp.where(column == wanted, 1.0, 0.0).astype(BF16)
    loads[0].wait()
    loads[1].wait()
    flat = jnp.concatenate([tk_ref[...].reshape(rows, hd), tv_ref[...].reshape(rows, hd)], axis=1)
    picked = dot(pick, flat).astype(BF16)
    for kv in range(2):
        tsend[kv] = picked[:, kv * hd : (kv + 1) * hd].reshape(heads, prompts, tokens, hd)

    pl.semaphore_wait(barrier, heads - 1 + groups - 1)

    tail_copies = ([], [])
    for kv in range(2):
        here = tail.at[kv, :, pl.ds(tp * tokens, tokens)]
        for d in range(1, heads):
            other = lax.rem(tp + d, heads)
            copy = pltpu.make_async_remote_copy(
                src_ref=tsend.at[kv, other],
                dst_ref=here,
                send_sem=tail_ssem.at[kv, d],
                recv_sem=tail_rsem.at[kv, d],
                device_id=(me, other),
                device_id_type=MESH,
            )
            copy.start()
            tail_copies[kv].append(copy)
        own = pltpu.make_async_copy(tsend.at[kv, tp], here, own_sem.at[kv])
        own.start()
        tail_copies[kv].append(own)

    loads[2].wait()
    dest_row = jnp.concatenate([dest_ref[p] for p in range(prompts)], axis=1)
    tab_v[...] = slot_table(dest_row, groups * SLOTS, blocks)
    table_copy = pltpu.make_async_copy(tab_v, tab_s, tab_sem)
    table_copy.start()
    chunk = tail_len
    chunks = whole_len // chunk
    loads[3].wait()
    starts = [len_ref[p] - tail_len for p in range(prompts)]
    distance = iota((chunk, tail_len), 0) - iota((chunk, tail_len), 1)
    for p in range(prompts):
        for c in range(chunks):
            shift[p, c] = jnp.where(distance == starts[p] - c * chunk, 1.0, 0.0).astype(BF16)
    wk[blocks] = jnp.zeros((BLOCK, hd), BF16)
    wv[blocks] = jnp.zeros((BLOCK, hd), BF16)
    table_copy.wait()

    local = []
    for kv, (whole, prefix) in enumerate(((wk, pk_ref), (wv, pv_ref))):
        loads[4 + kv].wait()
        for copy in tail_copies[kv]:
            copy.wait()
        for p in range(prompts):
            for c in range(chunks):
                moved = dot(shift[p, c], tail[kv, p])
                if c * chunk < prefix_len:
                    early = iota((chunk, hd), 0) + c * chunk < starts[p]
                    kept = prefix[p, c * chunk : (c + 1) * chunk].astype(F32)
                    moved = jnp.where(early, kept, moved)
                first = (p * whole_len + c * chunk) // BLOCK
                whole[first : first + chunk // BLOCK] = moved.astype(BF16).reshape(
                    chunk // BLOCK, BLOCK, hd
                )

        def pack(target):
            for r in range(SLOTS):
                send[kv, target, r] = whole[tab_s[0, target * SLOTS + r]]

        for dy in range(Y):

            def ship(dz, carry):
                target = partner(dy, dz)
                pack(target)
                pltpu.make_async_remote_copy(
                    src_ref=send.at[kv, target],
                    dst_ref=pool_ref.at[kv, me],
                    send_sem=ssem.at[kv],
                    recv_sem=rsem.at[kv],
                    device_id=(target, tp),
                    device_id_type=MESH,
                ).start()
                return carry

            lax.fori_loop(0 if dy else 1, nz, ship, 0)
        pack(me)
        own = pltpu.make_async_copy(send.at[kv, me], pool_ref.at[kv, me], own_sem.at[2 + kv])
        own.start()
        local.append(own)

    for load in loads[6:]:
        load.wait()
    scale = 1.0 / math.sqrt(hd)
    chunk_tokens = 32
    chunk_rows = chunk_tokens * group
    for p in range(prompts):
        length = len_ref[p]

        def keys_of(whole):
            return whole[p * per_prompt : (p + 1) * per_prompt].reshape(whole_len, hd)

        def prefill(c, carry):
            first = pl.multiple_of(c * chunk_tokens, chunk_tokens)
            q = q_ref[p, pl.ds(first, chunk_tokens)].reshape(chunk_rows, hd)
            scores = dot_t(q, keys_of(wk)) * scale
            token = lax.div(iota((chunk_rows, whole_len), 0), group)
            last = length - tail_len + first + token
            scores = jnp.where(iota((chunk_rows, whole_len), 1) <= last, scores, -jnp.inf)
            peak = jnp.max(scores, axis=1, keepdims=True)
            weights = jnp.exp(scores - peak)
            total = jnp.sum(weights, axis=1, keepdims=True)
            summed = dot(weights.astype(BF16), keys_of(wv))
            result = (summed / total).astype(BF16)
            out_ref[p, pl.ds(first, chunk_tokens)] = result.reshape(chunk_tokens, group, hd)
            return carry

        lax.fori_loop(0, tail_len // chunk_tokens, prefill, 0)

        steps = dq_ref.shape[1]
        dq = dq_ref[p].reshape(steps * group, hd)
        scores = dot_t(dq, keys_of(wk)) * scale
        scores = jnp.where(iota(scores.shape, 1) < length, scores, -jnp.inf)
        fresh = dot_t(dq, dk_ref[p]) * scale
        step = lax.div(iota(fresh.shape, 0), group)
        fresh = jnp.where(iota(fresh.shape, 1) <= step, fresh, -jnp.inf)
        peak = jnp.maximum(
            jnp.max(scores, axis=1, keepdims=True), jnp.max(fresh, axis=1, keepdims=True)
        )
        weights = jnp.exp(scores - peak)
        fresh_weights = jnp.exp(fresh - peak)
        total = jnp.sum(weights, axis=1, keepdims=True) + jnp.sum(
            fresh_weights, axis=1, keepdims=True
        )
        summed = dot(weights.astype(BF16), keys_of(wv))
        summed = summed + dot(fresh_weights.astype(BF16), dv_ref[p])
        dout_ref[p] = (summed / total).astype(BF16).reshape(steps, group, hd)

    for own in local:
        own.wait()
    for kv in range(2):
        others = pl.ds(0, groups - 1)
        every = pltpu.make_async_remote_copy(
            src_ref=send.at[kv, others],
            dst_ref=pool_ref.at[kv, others],
            send_sem=ssem.at[kv],
            recv_sem=rsem.at[kv],
            device_id=(partner(0, 1), tp),
            device_id_type=MESH,
        )
        every.wait_send()
        every.wait_recv()


def store_kernel(pool_ref, out_ref, dout_ref, pk_ref, pv_ref, o_ref, do_ref, sem):
    copies = [
        pltpu.make_async_copy(pool_ref.at[0], pk_ref, sem.at[0]),
        pltpu.make_async_copy(pool_ref.at[1], pv_ref, sem.at[1]),
        pltpu.make_async_copy(out_ref, o_ref, sem.at[2]),
        pltpu.make_async_copy(dout_ref, do_ref, sem.at[3]),
    ]
    for copy in copies:
        copy.start()
    for copy in copies:
        copy.wait()


def per_device(groups, heads, tq, tk, tv, pk, pv, dq, dk, dv, lengths, dest):
    prompts, tail_len, group, hd = tq.shape
    tokens = tk.shape[1]
    prefix_len = pk.shape[1]
    steps = dq.shape[1]
    blocks = prompts * (prefix_len + tail_len) // BLOCK
    vmem = pl.BlockSpec(memory_space=pltpu.VMEM)
    hbm = pl.BlockSpec(memory_space=pltpu.HBM)
    shape = jax.ShapeDtypeStruct
    operands = (
        tk,
        tv,
        dest.reshape(prompts, 1, dest.shape[1]),
        lengths,
        pk.reshape(prompts, prefix_len, hd),
        pv.reshape(prompts, prefix_len, hd),
        tq,
        dq,
        dk.reshape(prompts, steps, hd),
        dv.reshape(prompts, steps, hd),
    )
    held = [pltpu.VMEM(x.shape, x.dtype) for x in operands]
    held[3] = pltpu.SMEM(lengths.shape, lengths.dtype)
    out, dout, pool = pl.pallas_call(
        functools.partial(exchange_kernel, groups, heads),
        out_shape=(
            pltpu.VMEM(tq.shape, BF16),
            pltpu.VMEM(dq.shape, BF16),
            pltpu.VMEM((2, groups, SLOTS, BLOCK, hd), BF16),
        ),
        in_specs=[hbm] * len(operands),
        out_specs=(vmem, vmem, vmem),
        scratch_shapes=held
        + [
            pltpu.VMEM((2, heads, prompts, tokens, hd), BF16),
            pltpu.VMEM((2, prompts, tail_len, hd), BF16),
            pltpu.VMEM((prompts, (prefix_len + tail_len) // tail_len, tail_len, tail_len), BF16),
            pltpu.VMEM((blocks + 1, BLOCK, hd), BF16),
            pltpu.VMEM((blocks + 1, BLOCK, hd), BF16),
            pltpu.VMEM((2, groups, SLOTS, BLOCK, hd), BF16),
            pltpu.VMEM((1, groups * SLOTS), jnp.int32),
            pltpu.SMEM((1, groups * SLOTS), jnp.int32),
            pltpu.SemaphoreType.DMA((2, heads)),
            pltpu.SemaphoreType.DMA((2, heads)),
            pltpu.SemaphoreType.DMA((2,)),
            pltpu.SemaphoreType.DMA((2,)),
            pltpu.SemaphoreType.DMA,
            pltpu.SemaphoreType.DMA((4,)),
            pltpu.SemaphoreType.DMA((len(operands),)),
        ],
        compiler_params=pltpu.CompilerParams(
            collective_id=0, has_side_effects=True, vmem_limit_bytes=40 << 20
        ),
    )(*[pltpu.with_memory_space_constraint(x, pltpu.HBM) for x in operands])
    pool_k, pool_v, out, dout = pl.pallas_call(
        store_kernel,
        out_shape=(
            shape((groups, SLOTS, BLOCK, hd), BF16),
            shape((groups, SLOTS, BLOCK, hd), BF16),
            shape(tq.shape, BF16),
            shape(dq.shape, BF16),
        ),
        in_specs=[vmem] * 3,
        out_specs=(hbm,) * 4,
        scratch_shapes=[pltpu.SemaphoreType.DMA((4,))],
        compiler_params=pltpu.CompilerParams(vmem_limit_bytes=40 << 20),
    )(pool, out, dout)
    final = (1, groups * SLOTS, BLOCK, 1, hd)
    return out, dout, pool_k.reshape(final), pool_v.reshape(final)


def solution(mesh):
    in_specs = (
        P("req", None, "tp", None),
        P("req", "tp", None, None),
        P("req", "tp", None, None),
        P("req", None, "tp", None),
        P("req", None, "tp", None),
        P("req", None, "tp", None),
        P("req", None, "tp", None),
        P("req", None, "tp", None),
        P("req"),
        P("req", None, None),
    )
    out_specs = (
        P("req", None, "tp", None),
        P("req", None, "tp", None),
        P("req", None, None, "tp", None),
        P("req", None, None, "tp", None),
    )
    return jax.shard_map(
        functools.partial(per_device, mesh.shape["req"], mesh.shape["tp"]),
        mesh=mesh,
        in_specs=in_specs,
        out_specs=out_specs,
        check_vma=False,
    )
```

```python
import functools
import math

import jax
import jax.numpy as jnp
from jax import lax
from jax.experimental import pallas as pl
from jax.experimental.pallas import tpu as pltpu
from jax.sharding import PartitionSpec as P

MESH = pl.DeviceIdType.MESH
BLOCK = 16
SLOTS = 4
Y = 4
F32 = jnp.float32
BF16 = jnp.bfloat16


def iota(shape, dim):
    return lax.broadcasted_iota(jnp.int32, shape, dim)


def dot(a, b):
    return jnp.dot(a, b, preferred_element_type=F32)


def dot_t(a, b):
    return lax.dot_general(a, b, (((1,), (1,)), ((), ())), preferred_element_type=F32)


def slot_table(dest_row, slots, empty):
    count = dest_row.shape[1]
    by_lane = jnp.broadcast_to(dest_row, (count, count))
    by_row = by_lane.T
    earlier = iota((count, count), 1) < iota((count, count), 0)
    rank = jnp.sum(jnp.where((by_lane == by_row) & earlier, 1, 0), axis=1, keepdims=True)
    slot = by_row[:, :1] * SLOTS + rank
    held = slot == iota((count, slots), 1)
    block = iota((count, slots), 0) - empty
    return jnp.sum(jnp.where(held, block, 0), axis=0, keepdims=True) + empty


def exchange_kernel(
    groups,
    heads,
    tk_in,
    tv_in,
    dest_in,
    len_in,
    pk_in,
    pv_in,
    q_in,
    dq_in,
    dk_in,
    dv_in,
    out_ref,
    dout_ref,
    pool_ref,
    tk_ref,
    tv_ref,
    dest_ref,
    len_ref,
    pk_ref,
    pv_ref,
    q_ref,
    dq_ref,
    dk_ref,
    dv_ref,
    tsend,
    tail,
    shift,
    wk,
    wv,
    send,
    tab_v,
    tab_s,
    tail_ssem,
    tail_rsem,
    ssem,
    rsem,
    tab_sem,
    own_sem,
    isem,
):
    prompts, tail_len, group, hd = q_ref.shape
    tokens = tk_ref.shape[1]
    prefix_len = pk_ref.shape[1]
    whole_len = prefix_len + tail_len
    per_prompt = whole_len // BLOCK
    blocks = prompts * per_prompt
    me = lax.axis_index("req")
    tp = lax.axis_index("tp")
    nz = groups // Y
    my_y, my_z = me // nz, me % nz

    along_y = [lax.rem(my_y + dy, Y) * nz for dy in range(Y)]

    def partner(dy, dz):
        return along_y[dy] + lax.rem(my_z + dz, nz)

    loads = [
        pltpu.make_async_copy(source, target, isem.at[i])
        for i, (source, target) in enumerate(
            (
                (tk_in, tk_ref),
                (tv_in, tv_ref),
                (dest_in, dest_ref),
                (len_in, len_ref),
                (pk_in, pk_ref),
                (pv_in, pv_ref),
                (q_in, q_ref),
                (dq_in, dq_ref),
                (dk_in, dk_ref),
                (dv_in, dv_ref),
            )
        )
    ]
    for load in loads[:3]:
        load.start()

    barrier = pltpu.get_barrier_semaphore()
    for d in range(1, heads):
        other = lax.rem(tp + d, heads)
        pl.semaphore_signal(barrier, inc=1, device_id=(me, other), device_id_type=MESH)

    for dy in range(Y):
        for dz in range(nz):
            if dy or dz:
                pl.semaphore_signal(
                    barrier, inc=1, device_id=(partner(dy, dz), tp), device_id_type=MESH
                )
    for load in loads[3:]:
        load.start()

    rows = prompts * tokens * heads
    per_head = prompts * tokens
    row, column = iota((rows, rows), 0), iota((rows, rows), 1)
    wanted = (row & (per_head - 1)) * heads + (row >> (per_head.bit_length() - 1))
    pick = jnp.where(column == wanted, 1.0, 0.0).astype(BF16)

    def order_by_head(kv, source):
        loads[kv].wait()
        picked = dot(pick, source[...].reshape(rows, hd)).astype(BF16)
        tsend[kv] = picked.reshape(heads, prompts, tokens, hd)

    def send_tails(kv):
        here = tail.at[kv, :, pl.ds(tp * tokens, tokens)]
        copies = []
        for d in range(1, heads):
            other = lax.rem(tp + d, heads)
            copy = pltpu.make_async_remote_copy(
                src_ref=tsend.at[kv, other],
                dst_ref=here,
                send_sem=tail_ssem.at[kv, d],
                recv_sem=tail_rsem.at[kv, d],
                device_id=(me, other),
                device_id_type=MESH,
            )
            copy.start()
            copies.append(copy)
        own = pltpu.make_async_copy(tsend.at[kv, tp], here, own_sem.at[kv])
        own.start()
        return copies + [own]

    order_by_head(0, tk_ref)
    pl.semaphore_wait(barrier, heads - 1 + groups - 1)
    tail_copies = [send_tails(0)]
    order_by_head(1, tv_ref)
    tail_copies.append(send_tails(1))

    loads[2].wait()
    dest_row = jnp.concatenate([dest_ref[p] for p in range(prompts)], axis=1)
    tab_v[...] = slot_table(dest_row, groups * SLOTS, blocks)
    table_copy = pltpu.make_async_copy(tab_v, tab_s, tab_sem)
    table_copy.start()
    chunk = tail_len
    chunks = whole_len // chunk
    loads[3].wait()
    starts = [len_ref[p] - tail_len for p in range(prompts)]
    distance = iota((chunk, tail_len), 0) - iota((chunk, tail_len), 1)
    for p in range(prompts):
        for c in range(chunks):
            shift[p, c] = jnp.where(distance == starts[p] - c * chunk, 1.0, 0.0).astype(BF16)
    wk[blocks] = jnp.zeros((BLOCK, hd), BF16)
    wv[blocks] = jnp.zeros((BLOCK, hd), BF16)
    table_copy.wait()

    local = []
    for kv, (whole, prefix) in enumerate(((wk, pk_ref), (wv, pv_ref))):
        loads[4 + kv].wait()
        for copy in tail_copies[kv]:
            copy.wait()
        for p in range(prompts):
            for c in range(chunks):
                moved = dot(shift[p, c], tail[kv, p])
                if c * chunk < prefix_len:
                    early = iota((chunk, hd), 0) + c * chunk < starts[p]
                    kept = prefix[p, c * chunk : (c + 1) * chunk].astype(F32)
                    moved = jnp.where(early, kept, moved)
                first = (p * whole_len + c * chunk) // BLOCK
                whole[first : first + chunk // BLOCK] = moved.astype(BF16).reshape(
                    chunk // BLOCK, BLOCK, hd
                )

        def pack(target):
            for r in range(SLOTS):
                send[kv, target, r] = whole[tab_s[0, target * SLOTS + r]]

        for dy in (2, 1, 3, 0):

            def ship(dz, carry):
                target = partner(dy, dz)
                pack(target)
                pltpu.make_async_remote_copy(
                    src_ref=send.at[kv, target],
                    dst_ref=pool_ref.at[kv, me],
                    send_sem=ssem.at[kv],
                    recv_sem=rsem.at[kv],
                    device_id=(target, tp),
                    device_id_type=MESH,
                ).start()
                return carry

            lax.fori_loop(0 if dy else 1, nz, ship, 0)
        pack(me)
        own = pltpu.make_async_copy(send.at[kv, me], pool_ref.at[kv, me], own_sem.at[2 + kv])
        own.start()
        local.append(own)

    for load in loads[6:]:
        load.wait()
    scale = 1.0 / math.sqrt(hd)
    chunk_tokens = 32
    chunk_rows = chunk_tokens * group
    for p in range(prompts):
        length = len_ref[p]

        def keys_of(whole):
            return whole[p * per_prompt : (p + 1) * per_prompt].reshape(whole_len, hd)

        def prefill(c, carry):
            first = pl.multiple_of(c * chunk_tokens, chunk_tokens)
            q = q_ref[p, pl.ds(first, chunk_tokens)].reshape(chunk_rows, hd)
            scores = dot_t(q, keys_of(wk)) * scale
            token = lax.div(iota((chunk_rows, whole_len), 0), group)
            last = length - tail_len + first + token
            scores = jnp.where(iota((chunk_rows, whole_len), 1) <= last, scores, -jnp.inf)
            peak = jnp.max(scores, axis=1, keepdims=True)
            weights = jnp.exp(scores - peak)
            total = jnp.sum(weights, axis=1, keepdims=True)
            summed = dot(weights.astype(BF16), keys_of(wv))
            result = (summed / total).astype(BF16)
            out_ref[p, pl.ds(first, chunk_tokens)] = result.reshape(chunk_tokens, group, hd)
            return carry

        lax.fori_loop(0, tail_len // chunk_tokens, prefill, 0)

        steps = dq_ref.shape[1]
        dq = dq_ref[p].reshape(steps * group, hd)
        scores = dot_t(dq, keys_of(wk)) * scale
        scores = jnp.where(iota(scores.shape, 1) < length, scores, -jnp.inf)
        fresh = dot_t(dq, dk_ref[p]) * scale
        step = lax.div(iota(fresh.shape, 0), group)
        fresh = jnp.where(iota(fresh.shape, 1) <= step, fresh, -jnp.inf)
        peak = jnp.maximum(
            jnp.max(scores, axis=1, keepdims=True), jnp.max(fresh, axis=1, keepdims=True)
        )
        weights = jnp.exp(scores - peak)
        fresh_weights = jnp.exp(fresh - peak)
        total = jnp.sum(weights, axis=1, keepdims=True) + jnp.sum(
            fresh_weights, axis=1, keepdims=True
        )
        summed = dot(weights.astype(BF16), keys_of(wv))
        summed = summed + dot(fresh_weights.astype(BF16), dv_ref[p])
        dout_ref[p] = (summed / total).astype(BF16).reshape(steps, group, hd)

    for own in local:
        own.wait()
    for kv in range(2):
        others = pl.ds(0, groups - 1)
        every = pltpu.make_async_remote_copy(
            src_ref=send.at[kv, others],
            dst_ref=pool_ref.at[kv, others],
            send_sem=ssem.at[kv],
            recv_sem=rsem.at[kv],
            device_id=(partner(0, 1), tp),
            device_id_type=MESH,
        )
        every.wait_send()
        every.wait_recv()


def store_kernel(pool_ref, out_ref, dout_ref, pk_ref, pv_ref, o_ref, do_ref, sem):
    copies = [
        pltpu.make_async_copy(pool_ref.at[0], pk_ref, sem.at[0]),
        pltpu.make_async_copy(pool_ref.at[1], pv_ref, sem.at[1]),
        pltpu.make_async_copy(out_ref, o_ref, sem.at[2]),
        pltpu.make_async_copy(dout_ref, do_ref, sem.at[3]),
    ]
    for copy in copies:
        copy.start()
    for copy in copies:
        copy.wait()


def per_device(groups, heads, tq, tk, tv, pk, pv, dq, dk, dv, lengths, dest):
    prompts, tail_len, group, hd = tq.shape
    tokens = tk.shape[1]
    prefix_len = pk.shape[1]
    steps = dq.shape[1]
    blocks = prompts * (prefix_len + tail_len) // BLOCK
    vmem = pl.BlockSpec(memory_space=pltpu.VMEM)
    hbm = pl.BlockSpec(memory_space=pltpu.HBM)
    shape = jax.ShapeDtypeStruct
    operands = (
        tk,
        tv,
        dest.reshape(prompts, 1, dest.shape[1]),
        lengths,
        pk.reshape(prompts, prefix_len, hd),
        pv.reshape(prompts, prefix_len, hd),
        tq,
        dq,
        dk.reshape(prompts, steps, hd),
        dv.reshape(prompts, steps, hd),
    )
    held = [pltpu.VMEM(x.shape, x.dtype) for x in operands]
    held[3] = pltpu.SMEM(lengths.shape, lengths.dtype)
    out, dout, pool = pl.pallas_call(
        functools.partial(exchange_kernel, groups, heads),
        out_shape=(
            pltpu.VMEM(tq.shape, BF16),
            pltpu.VMEM(dq.shape, BF16),
            pltpu.VMEM((2, groups, SLOTS, BLOCK, hd), BF16),
        ),
        in_specs=[hbm] * len(operands),
        out_specs=(vmem, vmem, vmem),
        scratch_shapes=held
        + [
            pltpu.VMEM((2, heads, prompts, tokens, hd), BF16),
            pltpu.VMEM((2, prompts, tail_len, hd), BF16),
            pltpu.VMEM((prompts, (prefix_len + tail_len) // tail_len, tail_len, tail_len), BF16),
            pltpu.VMEM((blocks + 1, BLOCK, hd), BF16),
            pltpu.VMEM((blocks + 1, BLOCK, hd), BF16),
            pltpu.VMEM((2, groups, SLOTS, BLOCK, hd), BF16),
            pltpu.VMEM((1, groups * SLOTS), jnp.int32),
            pltpu.SMEM((1, groups * SLOTS), jnp.int32),
            pltpu.SemaphoreType.DMA((2, heads)),
            pltpu.SemaphoreType.DMA((2, heads)),
            pltpu.SemaphoreType.DMA((2,)),
            pltpu.SemaphoreType.DMA((2,)),
            pltpu.SemaphoreType.DMA,
            pltpu.SemaphoreType.DMA((4,)),
            pltpu.SemaphoreType.DMA((len(operands),)),
        ],
        compiler_params=pltpu.CompilerParams(
            collective_id=0, has_side_effects=True, vmem_limit_bytes=40 << 20
        ),
    )(*[pltpu.with_memory_space_constraint(x, pltpu.HBM) for x in operands])
    pool_k, pool_v, out, dout = pl.pallas_call(
        store_kernel,
        out_shape=(
            shape((groups, SLOTS, BLOCK, hd), BF16),
            shape((groups, SLOTS, BLOCK, hd), BF16),
            shape(tq.shape, BF16),
            shape(dq.shape, BF16),
        ),
        in_specs=[vmem] * 3,
        out_specs=(hbm,) * 4,
        scratch_shapes=[pltpu.SemaphoreType.DMA((4,))],
        compiler_params=pltpu.CompilerParams(vmem_limit_bytes=40 << 20),
    )(pool, out, dout)
    final = (1, groups * SLOTS, BLOCK, 1, hd)
    return out, dout, pool_k.reshape(final), pool_v.reshape(final)


def solution(mesh):
    in_specs = (
        P("req", None, "tp", None),
        P("req", "tp", None, None),
        P("req", "tp", None, None),
        P("req", None, "tp", None),
        P("req", None, "tp", None),
        P("req", None, "tp", None),
        P("req", None, "tp", None),
        P("req", None, "tp", None),
        P("req"),
        P("req", None, None),
    )
    out_specs = (
        P("req", None, "tp", None),
        P("req", None, "tp", None),
        P("req", None, None, "tp", None),
        P("req", None, None, "tp", None),
    )
    return jax.shard_map(
        functools.partial(per_device, mesh.shape["req"], mesh.shape["tp"]),
        mesh=mesh,
        in_specs=in_specs,
        out_specs=out_specs,
        check_vma=False,
    )
```

```python
import functools
import math

import jax
import jax.numpy as jnp
from jax import lax
from jax.experimental import pallas as pl
from jax.experimental.pallas import tpu as pltpu
from jax.sharding import PartitionSpec as P

MESH = pl.DeviceIdType.MESH
BLOCK = 16
SLOTS = 4
Y = 4
F32 = jnp.float32
BF16 = jnp.bfloat16


def iota(shape, dim):
    return lax.broadcasted_iota(jnp.int32, shape, dim)


def dot(a, b):
    return jnp.dot(a, b, preferred_element_type=F32)


def dot_t(a, b):
    return lax.dot_general(a, b, (((1,), (1,)), ((), ())), preferred_element_type=F32)


def slot_table(dest_row, slots, empty):
    count = dest_row.shape[1]
    by_lane = jnp.broadcast_to(dest_row, (count, count))
    by_row = by_lane.T
    earlier = iota((count, count), 1) < iota((count, count), 0)
    rank = jnp.sum(jnp.where((by_lane == by_row) & earlier, 1, 0), axis=1, keepdims=True)
    slot = by_row[:, :1] * SLOTS + rank
    held = slot == iota((count, slots), 1)
    block = iota((count, slots), 0) - empty
    return jnp.sum(jnp.where(held, block, 0), axis=0, keepdims=True) + empty


def exchange_kernel(
    groups,
    heads,
    tk_in,
    tv_in,
    dest_in,
    len_in,
    pk_in,
    pv_in,
    q_in,
    dq_in,
    dk_in,
    dv_in,
    out_ref,
    dout_ref,
    pool_ref,
    tk_ref,
    tv_ref,
    dest_ref,
    len_ref,
    pk_ref,
    pv_ref,
    q_ref,
    dq_ref,
    dk_ref,
    dv_ref,
    tsend,
    tail,
    shift,
    wk,
    wv,
    send,
    tab_v,
    tab_s,
    tail_ssem,
    tail_rsem,
    ssem,
    rsem,
    tab_sem,
    own_sem,
    isem,
):
    prompts, tail_len, group, hd = q_ref.shape
    tokens = tk_ref.shape[1]
    prefix_len = pk_ref.shape[1]
    whole_len = prefix_len + tail_len
    per_prompt = whole_len // BLOCK
    blocks = prompts * per_prompt
    me = lax.axis_index("req")
    tp = lax.axis_index("tp")
    nz = groups // Y
    my_y, my_z = me // nz, me % nz

    along_y = [lax.rem(my_y + dy, Y) * nz for dy in range(Y)]

    def partner(dy, dz):
        return along_y[dy] + lax.rem(my_z + dz, nz)

    loads = [
        pltpu.make_async_copy(source, target, isem.at[i])
        for i, (source, target) in enumerate(
            (
                (tk_in, tk_ref),
                (tv_in, tv_ref),
                (dest_in, dest_ref),
                (len_in, len_ref),
                (pk_in, pk_ref),
                (pv_in, pv_ref),
                (q_in, q_ref),
                (dq_in, dq_ref),
                (dk_in, dk_ref),
                (dv_in, dv_ref),
            )
        )
    ]
    for load in loads[:3]:
        load.start()

    barrier = pltpu.get_barrier_semaphore()
    for d in range(1, heads):
        other = lax.rem(tp + d, heads)
        pl.semaphore_signal(barrier, inc=1, device_id=(me, other), device_id_type=MESH)

    for dy in range(Y):
        for dz in range(nz):
            if dy or dz:
                pl.semaphore_signal(
                    barrier, inc=1, device_id=(partner(dy, dz), tp), device_id_type=MESH
                )
    for load in loads[3:]:
        load.start()

    rows = prompts * tokens * heads
    per_head = prompts * tokens
    row, column = iota((rows, rows), 0), iota((rows, rows), 1)
    wanted = (row & (per_head - 1)) * heads + (row >> (per_head.bit_length() - 1))
    pick = jnp.where(column == wanted, 1.0, 0.0).astype(BF16)

    def order_by_head(kv, source):
        loads[kv].wait()
        picked = dot(pick, source[...].reshape(rows, hd)).astype(BF16)
        tsend[kv] = picked.reshape(heads, prompts, tokens, hd)

    def send_tails(kv):
        here = tail.at[kv, :, pl.ds(tp * tokens, tokens)]
        copies = []
        for d in range(1, heads):
            other = lax.rem(tp + d, heads)
            copy = pltpu.make_async_remote_copy(
                src_ref=tsend.at[kv, other],
                dst_ref=here,
                send_sem=tail_ssem.at[kv, d],
                recv_sem=tail_rsem.at[kv, d],
                device_id=(me, other),
                device_id_type=MESH,
            )
            copy.start()
            copies.append(copy)
        own = pltpu.make_async_copy(tsend.at[kv, tp], here, own_sem.at[kv])
        own.start()
        return copies + [own]

    order_by_head(0, tk_ref)
    loads[2].wait()
    dest_row = jnp.concatenate([dest_ref[p] for p in range(prompts)], axis=1)
    tab_v[...] = slot_table(dest_row, groups * SLOTS, blocks)
    table_copy = pltpu.make_async_copy(tab_v, tab_s, tab_sem)
    table_copy.start()
    pl.semaphore_wait(barrier, heads - 1 + groups - 1)
    tail_copies = [send_tails(0)]
    order_by_head(1, tv_ref)
    tail_copies.append(send_tails(1))

    chunk = tail_len
    chunks = whole_len // chunk
    loads[3].wait()
    starts = [len_ref[p] - tail_len for p in range(prompts)]
    distance = iota((chunk, tail_len), 0) - iota((chunk, tail_len), 1)
    for p in range(prompts):
        for c in range(chunks):
            shift[p, c] = jnp.where(distance == starts[p] - c * chunk, 1.0, 0.0).astype(BF16)
    wk[blocks] = jnp.zeros((BLOCK, hd), BF16)
    wv[blocks] = jnp.zeros((BLOCK, hd), BF16)
    table_copy.wait()

    local = []
    for kv, (whole, prefix) in enumerate(((wk, pk_ref), (wv, pv_ref))):
        loads[4 + kv].wait()
        for copy in tail_copies[kv]:
            copy.wait()
        for p in range(prompts):
            for c in range(chunks):
                moved = dot(shift[p, c], tail[kv, p])
                if c * chunk < prefix_len:
                    early = iota((chunk, hd), 0) + c * chunk < starts[p]
                    kept = prefix[p, c * chunk : (c + 1) * chunk].astype(F32)
                    moved = jnp.where(early, kept, moved)
                first = (p * whole_len + c * chunk) // BLOCK
                whole[first : first + chunk // BLOCK] = moved.astype(BF16).reshape(
                    chunk // BLOCK, BLOCK, hd
                )

        def pack(target):
            for r in range(SLOTS):
                send[kv, target, r] = whole[tab_s[0, target * SLOTS + r]]

        for dy in (2, 1, 3, 0):

            def ship(dz, carry):
                target = partner(dy, dz)
                pack(target)
                pltpu.make_async_remote_copy(
                    src_ref=send.at[kv, target],
                    dst_ref=pool_ref.at[kv, me],
                    send_sem=ssem.at[kv],
                    recv_sem=rsem.at[kv],
                    device_id=(target, tp),
                    device_id_type=MESH,
                ).start()
                return carry

            lax.fori_loop(0 if dy else 1, nz, ship, 0)
        pack(me)
        own = pltpu.make_async_copy(send.at[kv, me], pool_ref.at[kv, me], own_sem.at[2 + kv])
        own.start()
        local.append(own)

    for load in loads[6:]:
        load.wait()
    scale = 1.0 / math.sqrt(hd)
    chunk_tokens = 32
    chunk_rows = chunk_tokens * group
    for p in range(prompts):
        length = len_ref[p]

        def keys_of(whole):
            return whole[p * per_prompt : (p + 1) * per_prompt].reshape(whole_len, hd)

        def prefill(c, carry):
            first = pl.multiple_of(c * chunk_tokens, chunk_tokens)
            q = q_ref[p, pl.ds(first, chunk_tokens)].reshape(chunk_rows, hd)
            scores = dot_t(q, keys_of(wk)) * scale
            token = lax.div(iota((chunk_rows, whole_len), 0), group)
            last = length - tail_len + first + token
            scores = jnp.where(iota((chunk_rows, whole_len), 1) <= last, scores, -jnp.inf)
            peak = jnp.max(scores, axis=1, keepdims=True)
            weights = jnp.exp(scores - peak)
            total = jnp.sum(weights, axis=1, keepdims=True)
            summed = dot(weights.astype(BF16), keys_of(wv))
            result = (summed / total).astype(BF16)
            out_ref[p, pl.ds(first, chunk_tokens)] = result.reshape(chunk_tokens, group, hd)
            return carry

        lax.fori_loop(0, tail_len // chunk_tokens, prefill, 0)

        steps = dq_ref.shape[1]
        dq = dq_ref[p].reshape(steps * group, hd)
        scores = dot_t(dq, keys_of(wk)) * scale
        scores = jnp.where(iota(scores.shape, 1) < length, scores, -jnp.inf)
        fresh = dot_t(dq, dk_ref[p]) * scale
        step = lax.div(iota(fresh.shape, 0), group)
        fresh = jnp.where(iota(fresh.shape, 1) <= step, fresh, -jnp.inf)
        peak = jnp.maximum(
            jnp.max(scores, axis=1, keepdims=True), jnp.max(fresh, axis=1, keepdims=True)
        )
        weights = jnp.exp(scores - peak)
        fresh_weights = jnp.exp(fresh - peak)
        total = jnp.sum(weights, axis=1, keepdims=True) + jnp.sum(
            fresh_weights, axis=1, keepdims=True
        )
        summed = dot(weights.astype(BF16), keys_of(wv))
        summed = summed + dot(fresh_weights.astype(BF16), dv_ref[p])
        dout_ref[p] = (summed / total).astype(BF16).reshape(steps, group, hd)

    for own in local:
        own.wait()
    for kv in range(2):
        others = pl.ds(0, groups - 1)
        every = pltpu.make_async_remote_copy(
            src_ref=send.at[kv, others],
            dst_ref=pool_ref.at[kv, others],
            send_sem=ssem.at[kv],
            recv_sem=rsem.at[kv],
            device_id=(partner(0, 1), tp),
            device_id_type=MESH,
        )
        every.wait_send()
        every.wait_recv()


def store_kernel(pool_ref, out_ref, dout_ref, pk_ref, pv_ref, o_ref, do_ref, sem):
    copies = [
        pltpu.make_async_copy(pool_ref.at[0], pk_ref, sem.at[0]),
        pltpu.make_async_copy(pool_ref.at[1], pv_ref, sem.at[1]),
        pltpu.make_async_copy(out_ref, o_ref, sem.at[2]),
        pltpu.make_async_copy(dout_ref, do_ref, sem.at[3]),
    ]
    for copy in copies:
        copy.start()
    for copy in copies:
        copy.wait()


def per_device(groups, heads, tq, tk, tv, pk, pv, dq, dk, dv, lengths, dest):
    prompts, tail_len, group, hd = tq.shape
    tokens = tk.shape[1]
    prefix_len = pk.shape[1]
    steps = dq.shape[1]
    blocks = prompts * (prefix_len + tail_len) // BLOCK
    vmem = pl.BlockSpec(memory_space=pltpu.VMEM)
    hbm = pl.BlockSpec(memory_space=pltpu.HBM)
    shape = jax.ShapeDtypeStruct
    operands = (
        tk,
        tv,
        dest.reshape(prompts, 1, dest.shape[1]),
        lengths,
        pk.reshape(prompts, prefix_len, hd),
        pv.reshape(prompts, prefix_len, hd),
        tq,
        dq,
        dk.reshape(prompts, steps, hd),
        dv.reshape(prompts, steps, hd),
    )
    held = [pltpu.VMEM(x.shape, x.dtype) for x in operands]
    held[3] = pltpu.SMEM(lengths.shape, lengths.dtype)
    out, dout, pool = pl.pallas_call(
        functools.partial(exchange_kernel, groups, heads),
        out_shape=(
            pltpu.VMEM(tq.shape, BF16),
            pltpu.VMEM(dq.shape, BF16),
            pltpu.VMEM((2, groups, SLOTS, BLOCK, hd), BF16),
        ),
        in_specs=[hbm] * len(operands),
        out_specs=(vmem, vmem, vmem),
        scratch_shapes=held
        + [
            pltpu.VMEM((2, heads, prompts, tokens, hd), BF16),
            pltpu.VMEM((2, prompts, tail_len, hd), BF16),
            pltpu.VMEM((prompts, (prefix_len + tail_len) // tail_len, tail_len, tail_len), BF16),
            pltpu.VMEM((blocks + 1, BLOCK, hd), BF16),
            pltpu.VMEM((blocks + 1, BLOCK, hd), BF16),
            pltpu.VMEM((2, groups, SLOTS, BLOCK, hd), BF16),
            pltpu.VMEM((1, groups * SLOTS), jnp.int32),
            pltpu.SMEM((1, groups * SLOTS), jnp.int32),
            pltpu.SemaphoreType.DMA((2, heads)),
            pltpu.SemaphoreType.DMA((2, heads)),
            pltpu.SemaphoreType.DMA((2,)),
            pltpu.SemaphoreType.DMA((2,)),
            pltpu.SemaphoreType.DMA,
            pltpu.SemaphoreType.DMA((4,)),
            pltpu.SemaphoreType.DMA((len(operands),)),
        ],
        compiler_params=pltpu.CompilerParams(
            collective_id=0, has_side_effects=True, vmem_limit_bytes=40 << 20
        ),
    )(*[pltpu.with_memory_space_constraint(x, pltpu.HBM) for x in operands])
    pool_k, pool_v, out, dout = pl.pallas_call(
        store_kernel,
        out_shape=(
            shape((groups, SLOTS, BLOCK, hd), BF16),
            shape((groups, SLOTS, BLOCK, hd), BF16),
            shape(tq.shape, BF16),
            shape(dq.shape, BF16),
        ),
        in_specs=[vmem] * 3,
        out_specs=(hbm,) * 4,
        scratch_shapes=[pltpu.SemaphoreType.DMA((4,))],
        compiler_params=pltpu.CompilerParams(vmem_limit_bytes=40 << 20),
    )(pool, out, dout)
    final = (1, groups * SLOTS, BLOCK, 1, hd)
    return out, dout, pool_k.reshape(final), pool_v.reshape(final)


def solution(mesh):
    in_specs = (
        P("req", None, "tp", None),
        P("req", "tp", None, None),
        P("req", "tp", None, None),
        P("req", None, "tp", None),
        P("req", None, "tp", None),
        P("req", None, "tp", None),
        P("req", None, "tp", None),
        P("req", None, "tp", None),
        P("req"),
        P("req", None, None),
    )
    out_specs = (
        P("req", None, "tp", None),
        P("req", None, "tp", None),
        P("req", None, None, "tp", None),
        P("req", None, None, "tp", None),
    )
    return jax.shard_map(
        functools.partial(per_device, mesh.shape["req"], mesh.shape["tp"]),
        mesh=mesh,
        in_specs=in_specs,
        out_specs=out_specs,
        check_vma=False,
    )
```
